512 devices in a mesh: term: 32 (over z_hi, y, core), sec: 16 (over x, z_lo).
Axes of the slice: x: 4, y: 4, z: 16 (z_hi: 4, z_lo: 4; z = z_hi * 4 + z_lo), core: 2. Of those that a mesh axis runs over, the one named last changes fastest.
Arguments:
- wavefunction: bfloat16 [16, 512, 512], P('sec', 'term'), may hold values from -6 to 6
- left_operator_blocks: bfloat16 [128, 16, 512, 512], P('term', 'sec'), may hold values from -0.5 to 0.5
- right_ops: bfloat16 [128, 16, 512, 512], P('term', 'sec'), may hold values from -0.046875 to 0.046875
- charge_shift: int32 [128], replicated, may hold values from -2 to 2, as said below
- assignment: int32 [128], P('term'), may hold values from 0 to 127, each once
- sector_size: int32 [16], replicated, may hold values from 128 to 512, as said below
Outputs:
- sigma: bfloat16 [16, 512, 512], P('sec', 'term')
The draws below stay inside these ranges and needn't reach their ends.
Inputs may be any that keep to these rules, and one draw needn't show every extreme that they name: `sector_size`: some sector has exactly 512 live rows. `assignment`: each term appears in exactly one slot. `charge_shift`: every offset from -2 to 2 is taken by at least 25 terms.
All inputs are finite; a program needn't handle non-finite values.
Results may differ from the reference program's by a relative error of at most 0.0049.
Values may be sent and summed in bfloat16 or wider, within the bound.
No kernel may reach another device: no remote copies, remote signals or barrier semaphores. Data moves between devices by JAX's collectives and lax.ppermute only.
A program may use at most 64 MiB of HBM per device.

```python
import jax
import jax.numpy as jnp
from jax import lax

BLK = 512
TERMS = 128
SECTORS = 16


def draw_sector_size(key, part):
    key = jax.random.fold_in(key, 7)
    first, second_factor = jax.random.split(key)
    sizes = jax.random.randint(first, (SECTORS,), BLK // 4, BLK + 1)
    where_full = jax.random.randint(second_factor, (), 0, SECTORS)
    return jnp.where(jnp.arange(SECTORS) == where_full, BLK, sizes).astype(jnp.int32)


def draw_charge_shift(key, part):
    key = jax.random.fold_in(key, 11)
    cycle = jnp.arange(TERMS, dtype=jnp.int32) % 5 - 2
    return jax.random.permutation(key, cycle).astype(jnp.int32)


def with_spikes(drawn, stream_key, source, target, parts, factor):
    owner, partner = [(jnp.arange(drawn.shape[axis_at]) // (drawn.shape[axis_at] // parts)).reshape([-1 if axis == axis_at else 1 for axis in range(drawn.ndim)]) for axis_at in (source, target)]
    chosen = jax.random.permutation(stream_key, parts)[partner]
    strong = (owner == chosen) | (owner == (partner + parts // 2) % parts)
    return jnp.where(strong, factor * drawn, drawn)


def levels(stream_key, dims, shards, smallest, high):
    def one(dim, shards_of):
        heights = jax.random.uniform(jax.random.fold_in(jax.random.fold_in(stream_key, 6), dim), (shards_of,), jnp.float32, smallest / len(shards), high / len(shards))
        return jnp.repeat(jnp.exp(heights), dims[dim] // shards_of).reshape((-1,) + (1,) * (len(dims) - dim - 1))

    level = one(*shards[0])
    for cut in shards[1:]:
        level = level * one(*cut)
    return level


def bell_draw(rng, extent, spread, limit, shards=(), held_as=jnp.bfloat16):
    array = spread * jax.random.normal(rng, extent, jnp.float32)
    if shards:
        array = array * levels(rng, extent, shards, -0.22, 0.18)
    return jnp.clip(array, -limit, limit).astype(held_as)


def bell_draw_with(key, shape, spread, bound, cuts, heavy, held_as=jnp.bfloat16):
    drawn = spread * jax.random.normal(key, shape, jnp.float32)
    if cuts:
        drawn = drawn * levels(key, shape, cuts, -0.22, 0.18)
    return jnp.clip(with_spikes(drawn, jax.random.fold_in(key, 3), *heavy), -bound, bound).astype(held_as)


def setup_inputs(seed: int = 0) -> dict:
    streams_of = jax.random.split(jax.random.key(seed), 7)
    return {
        "wavefunction": bell_draw(streams_of[0], (SECTORS, BLK, BLK), 1.0, 6.0, ((0, 16), (1, 32))),
        "left_operator_blocks": bell_draw_with(streams_of[1], (TERMS, SECTORS, BLK, BLK), BLK ** -0.5, 0.5, ((0, 32), (1, 16)), (0, 2, 32, 2.75)),
        "right_ops": bell_draw(streams_of[2], (TERMS, SECTORS, BLK, BLK), (BLK * TERMS // 4) ** -0.5, 0.046875, ((0, 32), (1, 16))),
        "charge_shift": draw_charge_shift(jax.random.fold_in(streams_of[6], 71), 0),
        "assignment": jax.random.permutation(streams_of[4], TERMS).astype(jnp.int32),
        "sector_size": draw_sector_size(jax.random.fold_in(streams_of[6], 71), 0),
    }


def active_term_mask(size, count):
    idx = jnp.arange(count, dtype=jnp.int32)
    return (idx[None, :, None] < size[:, None, None]) & (idx[None, None, :] < size[:, None, None])


def reference(wavefunction, left_operator_blocks, right_ops, charge_shift, assignment, sector_size):
    nsec = wavefunction.shape[0]
    nblk = wavefunction.shape[1]
    mask = active_term_mask(sector_size, nblk)
    live = jnp.where(mask, wavefunction, jnp.zeros_like(wavefunction))
    empty = jnp.zeros((2, nblk, nblk), jnp.bfloat16)
    padded = jnp.concatenate([empty, live, empty], axis=0)

    def accumulate_term_slot(total, items):
        lop, rop, term_id = items
        shift = charge_shift[term_id].astype(jnp.int32)
        source = lax.dynamic_slice_in_dim(padded, (shift + 2).astype(jnp.int32), nsec, 0)
        inner = jnp.einsum("sij,sjk->sik", lop.astype(jnp.float32), source.astype(jnp.float32)).astype(jnp.bfloat16)
        term = jnp.einsum("sik,slk->sil", inner.astype(jnp.float32), rop.astype(jnp.float32))
        return total + term, None

    start = jnp.zeros((nsec, nblk, nblk), jnp.float32)
    total, _ = lax.scan(accumulate_term_slot, start, (left_operator_blocks, right_ops, assignment))
    return jnp.where(mask, total, 0.0).astype(jnp.bfloat16)
```

```python
import functools

import jax
import jax.numpy as jnp
from jax import lax
from jax.experimental import pallas as pl
from jax.experimental.pallas import tpu as pltpu
from jax.sharding import Mesh
from jax.sharding import PartitionSpec as P

ZH, Y, CORE, X, ZL = 4, 4, 2, 4, 4
SECTORS = X * ZL
NEAR = 5
SLAB = 16
F32, BF16 = jnp.float32, jnp.bfloat16

SMEM = pl.BlockSpec(memory_space=pltpu.SMEM)
VMEM = pl.BlockSpec(memory_space=pltpu.VMEM)
MIB = 1 << 20


def own_sector():
    return lax.axis_index("x") * ZL + lax.axis_index("zl")


def live_mask(size, nblk):
    term = (lax.axis_index("zh") * Y + lax.axis_index("y")) * CORE + lax.axis_index("core")
    rows = term * SLAB + lax.broadcasted_iota(jnp.int32, (SLAB, nblk), 0)
    cols = lax.broadcasted_iota(jnp.int32, (SLAB, nblk), 1)
    return (rows < size) & (cols < size)


def spread_kernel(size_ref, slab_ref, out_ref):
    slab = slab_ref[0]
    mask = live_mask(size_ref[own_sector()], slab.shape[1])
    live = jnp.where(mask, slab.astype(F32), 0.0).astype(BF16)
    for copy in range(out_ref.shape[0]):
        out_ref[copy] = live


def pick_kernel(column_ref, beside_ref, out_ref):
    zl = lax.axis_index("zl")
    for place in range(NEAR):
        sector = zl + place - 2

        @pl.when((sector >= 0) & (sector < ZL))
        def _():
            block = column_ref[jnp.clip(sector, 0, ZL - 1)]
            for y in range(Y):
                out_ref[y, place] = block

        @pl.when((sector < 0) | (sector >= ZL))
        def _():
            block = beside_ref[jnp.clip(jnp.where(sector < 0, sector + 2, sector - ZL), 0, 1)]
            for y in range(Y):
                out_ref[y, place] = block


def product_kernel(shift_ref, assign_ref, mine_ref, other_ref, left_ref, right_ref, keep_ref, send_ref, blocks, total):
    core = lax.axis_index("core")
    nblk = left_ref.shape[-1]
    for y in range(Y):
        for place in range(NEAR):
            blocks[place, :, y, pl.ds(core, 1)] = mine_ref[y, place][:, None]
            blocks[place, :, y, pl.ds(1 - core, 1)] = other_ref[y, place][:, None]
    slots = left_ref.shape[0]
    for slot in range(slots):
        place = shift_ref[assign_ref[slot]] + 2
        source = blocks[place].reshape(nblk, nblk)
        inner = jnp.dot(left_ref[slot, 0], source, preferred_element_type=F32).astype(BF16)
        part = lax.dot_general(inner, right_ref[slot, 0], (((1,), (1,)), ((), ())), preferred_element_type=F32)
        part = part.reshape(total.shape)
        if slot == 0:
            total[...] = part
        else:
            total[...] += part
    keep_ref[...] = total[:, core]
    send_ref[...] = total[:, 1 - core].astype(BF16)


def join_kernel(keep_ref, got_ref, out_ref):
    out_ref[...] = (keep_ref[...] + got_ref[...].astype(F32)).astype(BF16)


def finish_kernel(size_ref, parts_ref, out_ref):
    nblk = parts_ref.shape[-1]
    total = jnp.sum(parts_ref[...].astype(F32), axis=0)
    mask = live_mask(size_ref[own_sector()], nblk)
    out_ref[0] = jnp.where(mask, total, 0.0).astype(BF16)


def call(kernel, out_shape, in_specs, scratch=(), flops=0, moved=MIB, limit=16 * MIB):
    many = isinstance(out_shape, (tuple, list))
    return pl.pallas_call(
        kernel,
        out_shape=out_shape,
        in_specs=in_specs,
        out_specs=tuple(VMEM for _ in out_shape) if many else VMEM,
        scratch_shapes=scratch,
        cost_estimate=pl.CostEstimate(flops=flops, bytes_accessed=moved, transcendentals=0),
        compiler_params=pltpu.CompilerParams(vmem_limit_bytes=limit),
    )


def shape(*dims, dtype=BF16):
    return jax.ShapeDtypeStruct(dims, dtype)


def next_x(block):
    route = []
    for x in range(X):
        for zl in range(ZL):
            to = x + 1 if zl < ZL // 2 else x - 1
            if 0 <= to < X:
                route.append((x * ZL + zl, to * ZL + zl))
    return lax.ppermute(block, ("x", "zl"), route)


def swap_core(block):
    return lax.ppermute(block, "core", [(0, 1), (1, 0)])


def body(wavefunction, left_operator_blocks, right_ops, charge_shift, assignment, sector_size):
    nblk = wavefunction.shape[2]
    slots = left_operator_blocks.shape[0]
    spread = call(spread_kernel, shape(ZL * ZH, SLAB, nblk), [SMEM, VMEM])(sector_size, wavefunction)
    column = lax.all_to_all(spread, ("zl", "zh"), 0, 0, tiled=True).reshape(ZL, ZH, SLAB, nblk)
    low = lax.axis_index("zl") < ZL // 2
    beside = next_x(jnp.where(low, column[2:], column[:2]))
    near = call(pick_kernel, shape(Y, NEAR, ZH, SLAB, nblk), [VMEM, VMEM])(column, beside)
    mine = lax.all_to_all(near, "y", 0, 0, tiled=True)
    other = swap_core(mine)
    keep, send = call(
        product_kernel,
        (shape(ZH * Y, SLAB, nblk, dtype=F32), shape(ZH * Y, SLAB, nblk)),
        [SMEM, SMEM, VMEM, VMEM, VMEM, VMEM],
        scratch=[
            pltpu.VMEM((NEAR, ZH, Y, CORE, SLAB, nblk), BF16),
            pltpu.VMEM((ZH * Y, CORE, SLAB, nblk), F32),
        ],
        flops=slots * 4 * nblk**3,
        moved=8 * MIB,
        limit=32 * MIB,
    )(charge_shift, assignment, mine, other, left_operator_blocks, right_ops)
    joined = call(join_kernel, shape(ZH * Y, SLAB, nblk), [VMEM, VMEM])(keep, swap_core(send))
    parts = lax.all_to_all(joined, ("zh", "y"), 0, 0, tiled=True)
    return call(finish_kernel, shape(1, SLAB, nblk), [SMEM, VMEM])(sector_size, parts)


def solution(mesh):
    grid = Mesh(mesh.devices.reshape(ZH, Y, CORE, X, ZL), ("zh", "y", "core", "x", "zl"))
    term, sec = ("zh", "y", "core"), ("x", "zl")
    placed = (
        P(sec, term, None),
        P(term, sec, None, None),
        P(term, sec, None, None),
        P(),
        P(term),
        P(),
    )
    return jax.shard_map(body, mesh=grid, in_specs=placed, out_specs=P(sec, term, None), check_vma=False)
```

```python
import functools

import jax
import jax.numpy as jnp
from jax import lax
from jax.experimental import pallas as pl
from jax.experimental.pallas import tpu as pltpu
from jax.sharding import Mesh
from jax.sharding import PartitionSpec as P

ZH, Y, CORE, X, ZL = 4, 4, 2, 4, 4
SECTORS = X * ZL
NEAR = 5
SLAB = 16
F32, BF16 = jnp.float32, jnp.bfloat16

SMEM = pl.BlockSpec(memory_space=pltpu.SMEM)
VMEM = pl.BlockSpec(memory_space=pltpu.VMEM)
MIB = 1 << 20


def own_sector():
    return lax.axis_index("x") * ZL + lax.axis_index("zl")


def live_mask(size, nblk):
    term = (lax.axis_index("zh") * Y + lax.axis_index("y")) * CORE + lax.axis_index("core")
    rows = term * SLAB + lax.broadcasted_iota(jnp.int32, (SLAB, nblk), 0)
    cols = lax.broadcasted_iota(jnp.int32, (SLAB, nblk), 1)
    return (rows < size) & (cols < size)


def outgoing_kernel(column_ref, out_ref):
    low = lax.axis_index("zl") < ZL // 2
    out_ref[...] = column_ref[pl.ds(jnp.where(low, 2, 0), 2)]


def pick_kernel(column_ref, beside_ref, out_ref):
    zl = lax.axis_index("zl")
    for place in range(NEAR):
        sector = zl + place - 2

        @pl.when((sector >= 0) & (sector < ZL))
        def _():
            block = column_ref[jnp.clip(sector, 0, ZL - 1)]
            for y in range(Y):
                out_ref[y, place] = block

        @pl.when((sector < 0) | (sector >= ZL))
        def _():
            block = beside_ref[jnp.clip(jnp.where(sector < 0, sector + 2, sector - ZL), 0, 1)]
            for y in range(Y):
                out_ref[y, place] = block


def product_kernel(size_ref, shift_ref, assign_ref, mine_ref, other_ref, left_ref, right_ref, keep_ref, send_ref, blocks, total):
    core = lax.axis_index("core")
    nblk = left_ref.shape[-1]
    dims = (ZH, SLAB, nblk)
    inside = lax.broadcasted_iota(jnp.int32, dims, 0) * (Y * CORE * SLAB) + lax.broadcasted_iota(jnp.int32, dims, 1)
    cols = lax.broadcasted_iota(jnp.int32, dims, 2)
    sizes = [size_ref[jnp.clip(own_sector() + place - 2, 0, SECTORS - 1)] for place in range(NEAR)]
    for y in range(Y):
        for ref, of in ((mine_ref, core), (other_ref, 1 - core)):
            reach = jnp.maximum(inside + (y * CORE + of) * SLAB, cols)
            for place in range(NEAR):
                live = jnp.where(reach < sizes[place], ref[y, place].astype(F32), 0.0)
                blocks[place, :, y, pl.ds(of, 1)] = live.astype(BF16)[:, None]
    slots = left_ref.shape[0]
    for slot in range(slots):
        place = shift_ref[assign_ref[slot]] + 2
        source = blocks[place].reshape(nblk, nblk)
        inner = jnp.dot(left_ref[slot, 0], source, preferred_element_type=F32).astype(BF16)
        part = lax.dot_general(inner, right_ref[slot, 0], (((1,), (1,)), ((), ())), preferred_element_type=F32)
        part = part.reshape(total.shape)
        if slot == 0:
            total[...] = part
        else:
            total[...] += part
    keep_ref[...] = total[:, core]
    send_ref[...] = total[:, 1 - core].astype(BF16)


def join_kernel(keep_ref, both_ref, out_ref):
    got = both_ref[1 - lax.axis_index("core")]
    out_ref[...] = (keep_ref[...] + got.astype(F32)).astype(BF16)


def finish_kernel(size_ref, parts_ref, out_ref):
    nblk = parts_ref.shape[-1]
    total = jnp.sum(parts_ref[...].astype(F32), axis=0)
    mask = live_mask(size_ref[own_sector()], nblk)
    out_ref[0] = jnp.where(mask, total, 0.0).astype(BF16)


def call(kernel, out_shape, in_specs, scratch=(), flops=0, moved=MIB, limit=4 * MIB):
    many = isinstance(out_shape, (tuple, list))
    return pl.pallas_call(
        kernel,
        out_shape=out_shape,
        in_specs=in_specs,
        out_specs=tuple(VMEM for _ in out_shape) if many else VMEM,
        scratch_shapes=scratch,
        cost_estimate=pl.CostEstimate(flops=flops, bytes_accessed=moved, transcendentals=0),
        compiler_params=pltpu.CompilerParams(vmem_limit_bytes=limit),
    )


def shape(*dims, dtype=BF16):
    return jax.ShapeDtypeStruct(dims, dtype)


def next_x(block):
    route = []
    for x in range(X):
        for zl in range(ZL):
            to = x + 1 if zl < ZL // 2 else x - 1
            if 0 <= to < X:
                route.append((x * ZL + zl, to * ZL + zl))
    return lax.ppermute(block, ("x", "zl"), route)


def swap_core(block):
    return lax.ppermute(block, "core", [(0, 1), (1, 0)])


def body(wavefunction, left_operator_blocks, right_ops, charge_shift, assignment, sector_size):
    nblk = wavefunction.shape[2]
    slots = left_operator_blocks.shape[0]
    spread = jnp.broadcast_to(wavefunction, (ZL * ZH, SLAB, nblk))
    column = lax.all_to_all(spread, ("zl", "zh"), 0, 0, tiled=True).reshape(ZL, ZH, SLAB, nblk)
    beside = next_x(call(outgoing_kernel, shape(2, ZH, SLAB, nblk), [VMEM])(column))
    near = call(pick_kernel, shape(Y, NEAR, ZH, SLAB, nblk), [VMEM, VMEM])(column, beside)
    mine = lax.all_to_all(near, "y", 0, 0, tiled=True)
    other = swap_core(mine)
    keep, send = call(
        product_kernel,
        (shape(ZH * Y, SLAB, nblk, dtype=F32), shape(ZH * Y, SLAB, nblk)),
        [SMEM, SMEM, SMEM, VMEM, VMEM, VMEM, VMEM],
        scratch=[
            pltpu.VMEM((NEAR, ZH, Y, CORE, SLAB, nblk), BF16),
            pltpu.VMEM((ZH * Y, CORE, SLAB, nblk), F32),
        ],
        flops=slots * 4 * nblk**3,
        moved=8 * MIB,
        limit=12 * MIB,
    )(sector_size, charge_shift, assignment, mine, other, left_operator_blocks, right_ops)
    joined = call(join_kernel, shape(ZH * Y, SLAB, nblk), [VMEM, VMEM])(keep, lax.all_gather(send, "core"))
    parts = lax.all_to_all(joined, ("zh", "y"), 0, 0, tiled=True)
    return call(finish_kernel, shape(1, SLAB, nblk), [SMEM, VMEM])(sector_size, parts)


def solution(mesh):
    grid = Mesh(mesh.devices.reshape(ZH, Y, CORE, X, ZL), ("zh", "y", "core", "x", "zl"))
    term, sec = ("zh", "y", "core"), ("x", "zl")
    placed = (
        P(sec, term, None),
        P(term, sec, None, None),
        P(term, sec, None, None),
        P(),
        P(term),
        P(),
    )
    return jax.shard_map(body, mesh=grid, in_specs=placed, out_specs=P(sec, term, None), check_vma=False)
```

```python
import functools

import jax
import jax.numpy as jnp
from jax import lax
from jax.experimental import pallas as pl
from jax.experimental.pallas import tpu as pltpu
from jax.sharding import Mesh
from jax.sharding import PartitionSpec as P

ZH, Y, CORE, X, ZL = 4, 4, 2, 4, 4
SECTORS = X * ZL
NEAR = 5
SLAB = 16
F32, BF16 = jnp.float32, jnp.bfloat16

SMEM = pl.BlockSpec(memory_space=pltpu.SMEM)
VMEM = pl.BlockSpec(memory_space=pltpu.VMEM)
MIB = 1 << 20


def own_sector():
    return lax.axis_index("x") * ZL + lax.axis_index("zl")


def outgoing_kernel(column_ref, out_ref):
    low = lax.axis_index("zl") < ZL // 2
    out_ref[...] = column_ref[pl.ds(jnp.where(low, 2, 0), 2)]


def pick_kernel(column_ref, beside_ref, out_ref):
    zl = lax.axis_index("zl")
    for place in range(NEAR):
        sector = zl + place - 2

        @pl.when((sector >= 0) & (sector < ZL))
        def _():
            block = column_ref[jnp.clip(sector, 0, ZL - 1)]
            for y in range(Y):
                out_ref[y, place] = block

        @pl.when((sector < 0) | (sector >= ZL))
        def _():
            block = beside_ref[jnp.clip(jnp.where(sector < 0, sector + 2, sector - ZL), 0, 1)]
            for y in range(Y):
                out_ref[y, place] = block


def product_kernel(size_ref, shift_ref, assign_ref, mine_ref, other_ref, left_ref, right_ref, keep_ref, send_ref, blocks, total):
    core = lax.axis_index("core")
    nblk = left_ref.shape[-1]
    dims = (ZH, SLAB, nblk)
    inside = lax.broadcasted_iota(jnp.int32, dims, 0) * (Y * CORE * SLAB) + lax.broadcasted_iota(jnp.int32, dims, 1)
    cols = lax.broadcasted_iota(jnp.int32, dims, 2)
    sizes = [size_ref[jnp.clip(own_sector() + place - 2, 0, SECTORS - 1)] for place in range(NEAR)]
    for y in range(Y):
        for ref, of in ((mine_ref, core), (other_ref, 1 - core)):
            reach = jnp.maximum(inside + (y * CORE + of) * SLAB, cols)
            for place in range(NEAR):
                block = ref[y, place]
                live = jnp.where(reach < sizes[place], block, jnp.zeros_like(block))
                blocks[place, :, y, pl.ds(of, 1)] = live[:, None]
    slots = left_ref.shape[0]
    for slot in range(slots):
        place = shift_ref[assign_ref[slot]] + 2
        source = blocks[place].reshape(nblk, nblk)
        inner = jnp.dot(left_ref[slot, 0], source, preferred_element_type=F32).astype(BF16)
        part = lax.dot_general(inner, right_ref[slot, 0], (((1,), (1,)), ((), ())), preferred_element_type=F32)
        part = part.reshape(total.shape)
        if slot == 0:
            total[...] = part
        else:
            total[...] += part
    dims = keep_ref.shape
    slab = lax.broadcasted_iota(jnp.int32, dims, 0) * (CORE * SLAB) + lax.broadcasted_iota(jnp.int32, dims, 1)
    cols = lax.broadcasted_iota(jnp.int32, dims, 2)
    for ref, of in ((keep_ref, core), (send_ref, 1 - core)):
        reach = jnp.maximum(slab + of * SLAB, cols)
        ref[...] = jnp.where(reach < sizes[2], total[:, of], 0.0).astype(ref.dtype)


def join_kernel(keep_ref, both_ref, out_ref):
    core = lax.axis_index("core")
    for place in range(ZH * Y):
        joined = keep_ref[place] + both_ref[1 - core, place].astype(F32)
        out_ref[jnp.where(core == 0, place, ZH * Y - 1 - place)] = joined.astype(BF16)


def finish_kernel(parts_ref, out_ref):
    out_ref[0] = jnp.sum(parts_ref[...].astype(F32), axis=0).astype(BF16)


def call(kernel, out_shape, in_specs, scratch=(), flops=0, moved=MIB, limit=4 * MIB):
    many = isinstance(out_shape, (tuple, list))
    return pl.pallas_call(
        kernel,
        out_shape=out_shape,
        in_specs=in_specs,
        out_specs=tuple(VMEM for _ in out_shape) if many else VMEM,
        scratch_shapes=scratch,
        cost_estimate=pl.CostEstimate(flops=flops, bytes_accessed=moved, transcendentals=0),
        compiler_params=pltpu.CompilerParams(vmem_limit_bytes=limit),
    )


def shape(*dims, dtype=BF16):
    return jax.ShapeDtypeStruct(dims, dtype)


def next_x(block):
    route = []
    for x in range(X):
        for zl in range(ZL):
            to = x + 1 if zl < ZL // 2 else x - 1
            if 0 <= to < X:
                route.append((x * ZL + zl, to * ZL + zl))
    return lax.ppermute(block, ("x", "zl"), route)


def mirrored(block, axes):
    members = range(0, block.shape[0] * CORE, CORE)
    groups = [list(members), [member + 1 for member in reversed(members)]]
    return lax.all_to_all(block, (*axes, "core"), 0, 0, tiled=True, axis_index_groups=groups)


def swap_core(block):
    return lax.ppermute(block, "core", [(0, 1), (1, 0)])


def body(wavefunction, left_operator_blocks, right_ops, charge_shift, assignment, sector_size):
    nblk = wavefunction.shape[2]
    slots = left_operator_blocks.shape[0]
    spread = jnp.broadcast_to(wavefunction, (ZL * ZH, SLAB, nblk))
    column = lax.all_to_all(spread, ("zl", "zh"), 0, 0, tiled=True).reshape(ZL, ZH, SLAB, nblk)
    beside = next_x(call(outgoing_kernel, shape(2, ZH, SLAB, nblk), [VMEM])(column))
    near = call(pick_kernel, shape(Y, NEAR, ZH, SLAB, nblk), [VMEM, VMEM])(column, beside)
    mine = lax.all_to_all(near, "y", 0, 0, tiled=True)
    other = swap_core(mine)
    keep, send = call(
        product_kernel,
        (shape(ZH * Y, SLAB, nblk, dtype=F32), shape(ZH * Y, SLAB, nblk)),
        [SMEM, SMEM, SMEM, VMEM, VMEM, VMEM, VMEM],
        scratch=[
            pltpu.VMEM((NEAR, ZH, Y, CORE, SLAB, nblk), BF16),
            pltpu.VMEM((ZH * Y, CORE, SLAB, nblk), F32),
        ],
        flops=slots * 4 * nblk**3,
        moved=8 * MIB,
        limit=12 * MIB,
    )(sector_size, charge_shift, assignment, mine, other, left_operator_blocks, right_ops)
    joined = call(join_kernel, shape(ZH * Y, SLAB, nblk), [VMEM, VMEM])(keep, lax.all_gather(send, "core"))
    parts = mirrored(joined, ("zh", "y"))
    return call(finish_kernel, shape(1, SLAB, nblk), [VMEM])(parts)


def solution(mesh):
    grid = Mesh(mesh.devices.reshape(ZH, Y, CORE, X, ZL), ("zh", "y", "core", "x", "zl"))
    term, sec = ("zh", "y", "core"), ("x", "zl")
    placed = (
        P(sec, term, None),
        P(term, sec, None, None),
        P(term, sec, None, None),
        P(),
        P(term),
        P(),
    )
    return jax.shard_map(body, mesh=grid, in_specs=placed, out_specs=P(sec, term, None), check_vma=False)
```

```python
import functools

import jax
import jax.numpy as jnp
from jax import lax
from jax.experimental import pallas as pl
from jax.experimental.pallas import tpu as pltpu
from jax.sharding import Mesh
from jax.sharding import PartitionSpec as P

ZH, Y, CORE, X, ZL = 4, 4, 2, 4, 4
SECTORS = X * ZL
NEAR = 5
GRAY = (0, 1, 3, 2)
SLAB = 16
F32, BF16 = jnp.float32, jnp.bfloat16

SMEM = pl.BlockSpec(memory_space=pltpu.SMEM)
VMEM = pl.BlockSpec(memory_space=pltpu.VMEM)
MIB = 1 << 20


def own_sector():
    return lax.axis_index("x") * ZL + lax.axis_index("zl")


def gray(place):
    return jnp.where(place < 2, place, 5 - place)


def seat(core, place):
    return jnp.where(core == 0, gray(place), 3 - gray(place))


def outgoing_kernel(column_ref, out_ref):
    low = lax.axis_index("zl") < ZL // 2
    for place in range(2):
        out_ref[place] = column_ref[seat(lax.axis_index("core"), jnp.where(low, 2, 0) + place)]


def pick_kernel(column_ref, beside_ref, out_ref):
    zl = lax.axis_index("zl")
    for place in range(NEAR):
        sector = zl + place - 2

        @pl.when((sector >= 0) & (sector < ZL))
        def _():
            block = column_ref[seat(lax.axis_index("core"), jnp.clip(sector, 0, ZL - 1))]
            for y in range(Y):
                out_ref[y, place] = block

        @pl.when((sector < 0) | (sector >= ZL))
        def _():
            block = beside_ref[jnp.clip(jnp.where(sector < 0, sector + 2, sector - ZL), 0, 1)]
            for y in range(Y):
                out_ref[y, place] = block


def product_kernel(size_ref, shift_ref, assign_ref, mine_ref, other_ref, left_ref, right_ref, keep_ref, send_ref, blocks, total):
    core = lax.axis_index("core")
    nblk = left_ref.shape[-1]
    row = lax.broadcasted_iota(jnp.int32, (SLAB, nblk), 0)
    cols = lax.broadcasted_iota(jnp.int32, (SLAB, nblk), 1)
    sizes = [size_ref[jnp.clip(own_sector() + place - 2, 0, SECTORS - 1)] for place in range(NEAR)]
    for ref, of in ((mine_ref, core), (other_ref, 1 - core)):
        for at in range(ZH):
            zh = jnp.where(of == 0, GRAY[at], GRAY[3 - at])
            for y in range(Y):
                reach = jnp.maximum(((zh * Y + y) * CORE + of) * SLAB + row, cols)
                for place in range(NEAR):
                    block = ref[GRAY[y], place, at]
                    live = jnp.where(reach < sizes[place], block, jnp.zeros_like(block))
                    blocks[place, pl.ds(zh, 1), y, pl.ds(of, 1)] = live[None, None]
    slots = left_ref.shape[0]
    for slot in range(slots):
        place = shift_ref[assign_ref[slot]] + 2
        source = blocks[place].reshape(nblk, nblk)
        inner = jnp.dot(left_ref[slot, 0], source, preferred_element_type=F32).astype(BF16)
        part = lax.dot_general(inner, right_ref[slot, 0], (((1,), (1,)), ((), ())), preferred_element_type=F32)
        part = part.reshape(total.shape)
        if slot == 0:
            total[...] = part
        else:
            total[...] += part
    dims = keep_ref.shape
    slab = lax.broadcasted_iota(jnp.int32, dims, 0) * (CORE * SLAB) + lax.broadcasted_iota(jnp.int32, dims, 1)
    cols = lax.broadcasted_iota(jnp.int32, dims, 2)
    for ref, of in ((keep_ref, core), (send_ref, 1 - core)):
        reach = jnp.maximum(slab + of * SLAB, cols)
        ref[...] = jnp.where(reach < sizes[2], total[:, of], 0.0).astype(ref.dtype)


def join_kernel(keep_ref, both_ref, out_ref):
    core = lax.axis_index("core")
    for zh in range(ZH):
        for y in range(Y):
            joined = keep_ref[zh * Y + y] + both_ref[1 - core, zh * Y + y].astype(F32)
            out_ref[seat(core, y) * ZH + seat(core, zh)] = joined.astype(BF16)


def finish_kernel(parts_ref, out_ref):
    out_ref[0] = jnp.sum(parts_ref[...].astype(F32), axis=0).astype(BF16)


def call(kernel, out_shape, in_specs, scratch=(), flops=0, moved=MIB, limit=4 * MIB):
    many = isinstance(out_shape, (tuple, list))
    return pl.pallas_call(
        kernel,
        out_shape=out_shape,
        in_specs=in_specs,
        out_specs=tuple(VMEM for _ in out_shape) if many else VMEM,
        scratch_shapes=scratch,
        cost_estimate=pl.CostEstimate(flops=flops, bytes_accessed=moved, transcendentals=0),
        compiler_params=pltpu.CompilerParams(vmem_limit_bytes=limit),
    )


def shape(*dims, dtype=BF16):
    return jax.ShapeDtypeStruct(dims, dtype)


def next_x(block):
    route = []
    for x in range(X):
        for zl in range(ZL):
            to = x + 1 if zl < ZL // 2 else x - 1
            if 0 <= to < X:
                route.append((x * ZL + zl, to * ZL + zl))
    return lax.ppermute(block, ("x", "zl"), route)


def exchange(block, outer, inner):
    order = [(a * 4 + b) * CORE for a in GRAY for b in GRAY]
    groups = [order, [member + 1 for member in reversed(order)]]
    return lax.all_to_all(block, (outer, inner, "core"), 0, 0, tiled=True, axis_index_groups=groups)


def exchange_y(block):
    groups = [[y * CORE + core for y in GRAY] for core in range(CORE)]
    return lax.all_to_all(block, ("y", "core"), 0, 0, tiled=True, axis_index_groups=groups)


def swap_core(block):
    return lax.ppermute(block, "core", [(0, 1), (1, 0)])


def body(wavefunction, left_operator_blocks, right_ops, charge_shift, assignment, sector_size):
    nblk = wavefunction.shape[2]
    slots = left_operator_blocks.shape[0]
    spread = jnp.broadcast_to(wavefunction, (ZL * ZH, SLAB, nblk))
    column = exchange(spread, "zl", "zh").reshape(ZL, ZH, SLAB, nblk)
    beside = next_x(call(outgoing_kernel, shape(2, ZH, SLAB, nblk), [VMEM])(column))
    near = call(pick_kernel, shape(Y, NEAR, ZH, SLAB, nblk), [VMEM, VMEM])(column, beside)
    mine = exchange_y(near)
    other = swap_core(mine)
    keep, send = call(
        product_kernel,
        (shape(ZH * Y, SLAB, nblk, dtype=F32), shape(ZH * Y, SLAB, nblk)),
        [SMEM, SMEM, SMEM, VMEM, VMEM, VMEM, VMEM],
        scratch=[
            pltpu.VMEM((NEAR, ZH, Y, CORE, SLAB, nblk), BF16),
            pltpu.VMEM((ZH * Y, CORE, SLAB, nblk), F32),
        ],
        flops=slots * 4 * nblk**3,
        moved=8 * MIB,
        limit=12 * MIB,
    )(sector_size, charge_shift, assignment, mine, other, left_operator_blocks, right_ops)
    joined = call(join_kernel, shape(ZH * Y, SLAB, nblk), [VMEM, VMEM])(keep, lax.all_gather(send, "core"))
    parts = exchange(joined, "y", "zh")
    return call(finish_kernel, shape(1, SLAB, nblk), [VMEM])(parts)


def solution(mesh):
    grid = Mesh(mesh.devices.reshape(ZH, Y, CORE, X, ZL), ("zh", "y", "core", "x", "zl"))
    term, sec = ("zh", "y", "core"), ("x", "zl")
    placed = (
        P(sec, term, None),
        P(term, sec, None, None),
        P(term, sec, None, None),
        P(),
        P(term),
        P(),
    )
    return jax.shard_map(body, mesh=grid, in_specs=placed, out_specs=P(sec, term, None), check_vma=False)
```

```python
import functools

import jax
import jax.numpy as jnp
from jax import lax
from jax.experimental import pallas as pl
from jax.experimental.pallas import tpu as pltpu
from jax.sharding import Mesh
from jax.sharding import PartitionSpec as P

ZH, Y, CORE, X, ZL = 4, 4, 2, 4, 4
SECTORS = X * ZL
NEAR = 5
GRAY = (0, 1, 3, 2)
SLAB = 16
F32, BF16 = jnp.float32, jnp.bfloat16

SMEM = pl.BlockSpec(memory_space=pltpu.SMEM)
VMEM = pl.BlockSpec(memory_space=pltpu.VMEM)
MIB = 1 << 20


def own_sector():
    return lax.axis_index("x") * ZL + lax.axis_index("zl")


def gray(place):
    return jnp.where(place < 2, place, 5 - place)


def seat(core, place):
    return jnp.where(core == 0, gray(place), 3 - gray(place))


def outgoing_kernel(column_ref, out_ref):
    low = lax.axis_index("zl") < ZL // 2
    for place in range(2):
        out_ref[place] = column_ref[seat(lax.axis_index("core"), jnp.where(low, 2, 0) + place)]


def pick_kernel(column_ref, beside_ref, out_ref):
    zl = lax.axis_index("zl")
    for place in range(NEAR):
        sector = zl + place - 2

        @pl.when((sector >= 0) & (sector < ZL))
        def _():
            block = column_ref[seat(lax.axis_index("core"), jnp.clip(sector, 0, ZL - 1))]
            for y in range(Y):
                out_ref[y, place] = block

        @pl.when((sector < 0) | (sector >= ZL))
        def _():
            block = beside_ref[jnp.clip(jnp.where(sector < 0, sector + 2, sector - ZL), 0, 1)]
            for y in range(Y):
                out_ref[y, place] = block


def product_kernel(size_ref, shift_ref, assign_ref, mine_ref, other_ref, left_ref, right_ref, keep_ref, send_ref, blocks, total):
    core = lax.axis_index("core")
    nblk = left_ref.shape[-1]
    row = lax.broadcasted_iota(jnp.int32, (SLAB, nblk), 0)
    cols = lax.broadcasted_iota(jnp.int32, (SLAB, nblk), 1)
    sizes = [size_ref[jnp.clip(own_sector() + place - 2, 0, SECTORS - 1)] for place in range(NEAR)]
    for ref, of in ((mine_ref, core), (other_ref, 1 - core)):
        for at in range(ZH):
            zh = jnp.where(of == 0, GRAY[at], GRAY[3 - at])
            for y in range(Y):
                reach = jnp.maximum(((zh * Y + y) * CORE + of) * SLAB + row, cols)
                for place in range(NEAR):
                    block = ref[GRAY[y], place, at]
                    live = jnp.where(reach < sizes[place], block, jnp.zeros_like(block))
                    blocks[place, pl.ds(zh, 1), y, pl.ds(of, 1)] = live[None, None]
    slots = left_ref.shape[0]
    for slot in range(slots):
        place = shift_ref[assign_ref[slot]] + 2
        source = blocks[place].reshape(nblk, nblk)
        inner = jnp.dot(left_ref[slot, 0], source, preferred_element_type=F32).astype(BF16)
        part = lax.dot_general(inner, right_ref[slot, 0], (((1,), (1,)), ((), ())), preferred_element_type=F32)
        part = part.reshape(total.shape)
        if slot == 0:
            total[...] = part
        else:
            total[...] += part
    dims = keep_ref.shape
    slab = lax.broadcasted_iota(jnp.int32, dims, 0) * (CORE * SLAB) + lax.broadcasted_iota(jnp.int32, dims, 1)
    cols = lax.broadcasted_iota(jnp.int32, dims, 2)
    for ref, of in ((keep_ref, core), (send_ref, 1 - core)):
        reach = jnp.maximum(slab + of * SLAB, cols)
        ref[...] = jnp.where(reach < sizes[2], total[:, of], 0.0).astype(ref.dtype)


def join_kernel(keep_ref, both_ref, out_ref):
    core = lax.axis_index("core")
    for zh in range(ZH):
        for y in range(Y):
            joined = keep_ref[zh * Y + y] + both_ref[1 - core, zh * Y + y].astype(F32)
            place = jnp.where(core == 0, GRAY[y] * ZH + GRAY[zh], ZH * Y - 1 - (GRAY[zh] * Y + GRAY[y]))
            out_ref[place] = joined.astype(BF16)


def finish_kernel(parts_ref, out_ref):
    out_ref[0] = jnp.sum(parts_ref[...].astype(F32), axis=0).astype(BF16)


def call(kernel, out_shape, in_specs, scratch=(), flops=0, moved=MIB, limit=4 * MIB):
    many = isinstance(out_shape, (tuple, list))
    return pl.pallas_call(
        kernel,
        out_shape=out_shape,
        in_specs=in_specs,
        out_specs=tuple(VMEM for _ in out_shape) if many else VMEM,
        scratch_shapes=scratch,
        cost_estimate=pl.CostEstimate(flops=flops, bytes_accessed=moved, transcendentals=0),
        compiler_params=pltpu.CompilerParams(vmem_limit_bytes=limit),
    )


def shape(*dims, dtype=BF16):
    return jax.ShapeDtypeStruct(dims, dtype)


def next_x(block):
    route = []
    for x in range(X):
        for zl in range(ZL):
            to = x + 1 if zl < ZL // 2 else x - 1
            if 0 <= to < X:
                route.append((x * ZL + zl, to * ZL + zl))
    return lax.ppermute(block, ("x", "zl"), route)


def exchange(block, outer, inner, turned=False):
    order = [(a * 4 + b) * CORE for a in GRAY for b in GRAY]
    other = [(a * 4 + b) * CORE for b in GRAY for a in GRAY] if turned else order
    groups = [order, [member + 1 for member in reversed(other)]]
    return lax.all_to_all(block, (outer, inner, "core"), 0, 0, tiled=True, axis_index_groups=groups)


def exchange_y(block):
    groups = [[y * CORE + core for y in GRAY] for core in range(CORE)]
    return lax.all_to_all(block, ("y", "core"), 0, 0, tiled=True, axis_index_groups=groups)


def swap_core(block):
    return lax.ppermute(block, "core", [(0, 1), (1, 0)])


def body(wavefunction, left_operator_blocks, right_ops, charge_shift, assignment, sector_size):
    nblk = wavefunction.shape[2]
    slots = left_operator_blocks.shape[0]
    spread = jnp.broadcast_to(wavefunction, (ZL * ZH, SLAB, nblk))
    column = exchange(spread, "zl", "zh").reshape(ZL, ZH, SLAB, nblk)
    beside = next_x(call(outgoing_kernel, shape(2, ZH, SLAB, nblk), [VMEM])(column))
    near = call(pick_kernel, shape(Y, NEAR, ZH, SLAB, nblk), [VMEM, VMEM])(column, beside)
    mine = exchange_y(near)
    other = swap_core(mine)
    keep, send = call(
        product_kernel,
        (shape(ZH * Y, SLAB, nblk, dtype=F32), shape(ZH * Y, SLAB, nblk)),
        [SMEM, SMEM, SMEM, VMEM, VMEM, VMEM, VMEM],
        scratch=[
            pltpu.VMEM((NEAR, ZH, Y, CORE, SLAB, nblk), BF16),
            pltpu.VMEM((ZH * Y, CORE, SLAB, nblk), F32),
        ],
        flops=slots * 4 * nblk**3,
        moved=8 * MIB,
        limit=12 * MIB,
    )(sector_size, charge_shift, assignment, mine, other, left_operator_blocks, right_ops)
    joined = call(join_kernel, shape(ZH * Y, SLAB, nblk), [VMEM, VMEM])(keep, lax.all_gather(send, "core"))
    parts = exchange(joined, "y", "zh", turned=True)
    return call(finish_kernel, shape(1, SLAB, nblk), [VMEM])(parts)


def solution(mesh):
    grid = Mesh(mesh.devices.reshape(ZH, Y, CORE, X, ZL), ("zh", "y", "core", "x", "zl"))
    term, sec = ("zh", "y", "core"), ("x", "zl")
    placed = (
        P(sec, term, None),
        P(term, sec, None, None),
        P(term, sec, None, None),
        P(),
        P(term),
        P(),
    )
    return jax.shard_map(body, mesh=grid, in_specs=placed, out_specs=P(sec, term, None), check_vma=False)
```
